32 devices in a mesh: energy: 8 (over y, x, core), space: 4 (over z).
Axes of the slice: x: 2, y: 2, z: 4, core: 2. Of those that a mesh axis runs over, the one named last changes fastest.
Arguments:
- chain_map: float32 [2, 1536, 384], P(None, 'space'), may hold values from -0.21875 to 0.21875
- chain_source: float32 [2, 256, 1536], P(None, 'energy', 'space'), may hold values from -4 to 4
- local_map: float32 [2, 1536, 768], P(None, 'space'), may hold values from -0.21875 to 0.21875
- local_source: float32 [2, 3072, 256], P(None, 'space', 'energy'), may hold values from -6 to 6
- interaction: float32 [2, 4096, 256], P(None, 'space', 'energy'), may hold values from -6 to 6
- element_pairs: int32 [2, 4096], P(None, 'space'), may hold values from 0 to 767, as said below
Outputs:
- self_energy: float32 [2, 4096, 256], P(None, 'space', 'energy')
The draws below stay inside these ranges and needn't reach their ends.
Inputs may be any that keep to these rules, and one draw needn't show every extreme that they name: `element_pairs`: both orbitals of a selected element lie in the same block of 384 orbitals or in neighbouring blocks of its partition.
All inputs are finite; a program needn't handle non-finite values.
Results may differ from the reference program's by a relative error of at most 0.00011.
Values sent between devices are 32-bit elements; how exact they have to be, the bound alone decides.
A program may use at most 64 MiB of HBM per device.

```python
import jax
import jax.numpy as jnp
from jax import lax

B = 384
LBLK = 2
NSEL_DEV = 1024
LOC = 768
NCHAIN = 1536
NORB = 3072
NE = 256
NSEL_ALL = 4096
N_SPACE = 4


def draw_element_pairs(key, part):
    first_key, step_key, inner_key = jax.random.split(jax.random.fold_in(key, 17), 3)
    first_orbital = jax.random.randint(first_key, (NSEL_ALL,), 0, LOC)
    offsets = jax.random.randint(step_key, (NSEL_ALL,), -1, 2)
    second_block = jnp.clip(first_orbital // B + offsets, 0, LBLK - 1)
    second_orbital = second_block * B + jax.random.randint(inner_key, (NSEL_ALL,), 0, B)
    return jnp.stack([first_orbital, second_orbital]).astype(jnp.int32)


def levels(stream_key, extent, cuts, low, high):
    def one(axis_at, shards_of):
        steps = jax.random.uniform(jax.random.fold_in(jax.random.fold_in(stream_key, 6), axis_at), (shards_of,), jnp.float32, low / len(cuts), high / len(cuts))
        return jnp.repeat(jnp.exp(steps), extent[axis_at] // shards_of).reshape((-1,) + (1,) * (len(extent) - axis_at - 1))

    gain = one(*cuts[0])
    for cut in cuts[1:]:
        gain = gain * one(*cut)
    return gain


def centred(stream_key, shape, width, bound, shards=(), kind=jnp.bfloat16):
    values = width * jax.random.normal(stream_key, shape, jnp.float32)
    if shards:
        values = values * levels(stream_key, shape, shards, -0.22, 0.18)
    return jnp.clip(values, -bound, bound).astype(kind)


def setup_inputs(seed: int = 0) -> dict:
    arg_keys = jax.random.split(jax.random.key(seed), 7)
    return {
        "chain_map": centred(arg_keys[0], (2, NCHAIN, B), (2 * B) ** -0.5, 0.21875, ((1, 4),), jnp.float32),
        "chain_source": centred(arg_keys[1], (2, NE, NCHAIN), 0.25, 4.0, ((1, 8), (2, 4)), jnp.float32),
        "local_map": centred(arg_keys[2], (2, NCHAIN, LOC), (2 * B) ** -0.5, 0.21875, ((1, 4),), jnp.float32),
        "local_source": centred(arg_keys[3], (2, NORB, NE), 0.5, 6.0, ((1, 4), (2, 8)), jnp.float32),
        "interaction": centred(arg_keys[4], (2, NSEL_ALL, NE), 1.0, 6.0, ((1, 4), (2, 8)), jnp.float32),
        "element_pairs": draw_element_pairs(jax.random.fold_in(arg_keys[6], 71), 0),
    }


highest = lax.Precision.HIGHEST


def plain_dot(left_part, right_part):
    return jnp.dot(left_part, right_part, precision=highest, preferred_element_type=jnp.float32)


def across_dot(left_part, right_part):
    return lax.dot_general(left_part, right_part, (((0,), (1,)), ((), ())), precision=highest, preferred_element_type=jnp.float32)


def reference(chain_map, chain_source, local_map, local_source, interaction, element_pairs):
    state_re = jnp.zeros((NE, B), jnp.float32)
    state_im = jnp.zeros((NE, B), jnp.float32)
    pieces = []
    for partition in range(N_SPACE):
        chain_start = partition * B
        chain_stop = chain_start + B
        orbital_start = partition * LOC
        orbital_stop = orbital_start + LOC
        select_start = partition * NSEL_DEV
        select_stop = select_start + NSEL_DEV
        back_re = local_map[0, chain_start:chain_stop]
        back_im = local_map[1, chain_start:chain_stop]
        wave_re = across_dot(back_re, state_re) - across_dot(back_im, state_im) + local_source[0, orbital_start:orbital_stop]
        wave_im = across_dot(back_re, state_im) + across_dot(back_im, state_re) + local_source[1, orbital_start:orbital_stop]
        first_orbital = element_pairs[0, select_start:select_stop]
        second_orbital = element_pairs[1, select_start:select_stop]
        left_re = wave_re[first_orbital]
        left_im = wave_im[first_orbital]
        right_re = wave_re[second_orbital]
        right_im = wave_im[second_orbital]
        lesser_re = left_re * right_re + left_im * right_im
        lesser_im = left_im * right_re - left_re * right_im
        screened = interaction[0, select_start:select_stop] + 1j * interaction[1, select_start:select_stop]
        spectrum = jnp.fft.fft(lesser_re + 1j * lesser_im, axis=1) * jnp.fft.fft(screened, axis=1)
        response = jnp.fft.ifft(spectrum, axis=1) * (NE ** -0.5)
        pieces.append(jnp.stack([jnp.real(response), jnp.imag(response)]).astype(jnp.float32))
        coupling_re = chain_map[0, chain_start:chain_stop]
        coupling_im = chain_map[1, chain_start:chain_stop]
        new_re = plain_dot(state_re, coupling_re) - plain_dot(state_im, coupling_im) + chain_source[0, :, chain_start:chain_stop]
        new_im = plain_dot(state_re, coupling_im) + plain_dot(state_im, coupling_re) + chain_source[1, :, chain_start:chain_stop]
        state_re = new_re
        state_im = new_im
    return jnp.concatenate(pieces, axis=1)
```

```python
import functools
import math

import jax
import jax.numpy as jnp
import ml_dtypes
import numpy as np
from jax import lax
from jax.experimental import pallas as pl
from jax.experimental.pallas import tpu as pltpu
from jax.sharding import PartitionSpec as P

LANES = 128
RADIX = 256
MESH = pl.DeviceIdType.MESH
bf16, f32 = jnp.bfloat16, jnp.float32


def split(x):
    high = x.astype(bf16)
    return high, (x - high.astype(f32)).astype(bf16)


def mm(a, b):
    return jnp.dot(a, b, preferred_element_type=f32)


def transform_tables(length):
    inner = min(length, RADIX)
    index = np.arange(inner)
    angle = 2.0 * np.pi / inner * (np.outer(index, index) % inner)
    table = np.concatenate([np.cos(angle), np.sin(angle)], axis=0).astype(np.float32)
    high = table.astype(ml_dtypes.bfloat16)
    low = (table - high.astype(np.float32)).astype(ml_dtypes.bfloat16)
    return np.concatenate([high, high, low], axis=1)


def small_transform(table, x, sign):
    inner, width = x.shape[0], x.shape[1] // 2
    high, low = split(x)
    product = mm(table, jnp.concatenate([high, low, high], axis=0))
    cos, sin = product[:inner], product[inner:]
    re = cos[:, :width] - sign * sin[:, width:]
    im = cos[:, width:] + sign * sin[:, :width]
    return re, im


def twiddle(k, inner, length, sign):
    row = lax.broadcasted_iota(jnp.int32, (inner, 1), 0)
    angle = (sign * 2.0 * math.pi / length) * ((row * k) % length).astype(f32)
    return jnp.cos(angle), jnp.sin(angle)


def combine(parts, k, sign):
    total_re = total_im = None
    for a, (re, im) in enumerate(parts):
        angle = sign * 2.0 * math.pi * (a * k % len(parts)) / len(parts)
        c, s = math.cos(angle), math.sin(angle)
        one_re, one_im = c * re - s * im, c * im + s * re
        total_re = one_re if a == 0 else total_re + one_re
        total_im = one_im if a == 0 else total_im + one_im
    return total_re, total_im


def forward(table, parts, length):
    outer, inner = len(parts), parts[0][0].shape[0]
    out = []
    for k in range(outer):
        re, im = parts[0] if outer == 1 else combine(parts, k, -1.0)
        if k:
            c, s = twiddle(k, inner, length, -1.0)
            re, im = c * re - s * im, c * im + s * re
        out.append(small_transform(table, jnp.concatenate([re, im], axis=1), -1.0))
    return out


def inverse(table, spectra, length):
    outer, inner = len(spectra), spectra[0][0].shape[0]
    parts = []
    for k, (re, im) in enumerate(spectra):
        re, im = small_transform(table, jnp.concatenate([re, im], axis=1), 1.0)
        if k:
            c, s = twiddle(k, inner, length, 1.0)
            re, im = c * re - s * im, c * im + s * re
        parts.append((re, im))
    if outer == 1:
        return parts
    return [combine(parts, a, 1.0) for a in range(outer)]


def apply_map(states, high_ref, low_ref):
    count = states.shape[0] // 2
    high, low = split(states)
    rows = jnp.concatenate([high, low], axis=0)
    planes = []
    for plane in range(2):
        p = mm(rows, high_ref[plane])
        planes.append(p[: 2 * count] + p[2 * count :] + mm(high, low_ref[plane]))
    re = planes[0][:count] - planes[1][count:]
    im = planes[1][:count] + planes[0][count:]
    return re, im


def kernel(
    groups, space,
    chain_hbm, source_ref, map_hbm, local_ref, inter_ref, pairs_ref, table_hbm,
    out_ref,
    chain_f, map_f, table, chain_hi, chain_lo, map_hi, map_lo, onehot,
    incoming, outgoing, i_stage, i_recv, l_stage, l_recv, r_stage, r_recv,
    load_sem, hop_send, hop_recv, i_send, i_got, l_send, l_got, r_send, r_got,
):
    me = lax.axis_index("energy")
    z = lax.axis_index("space")
    count = source_ref.shape[1]
    width = local_ref.shape[2]
    selected = inter_ref.shape[2]
    piece = selected // groups
    chunk = l_stage.shape[3]
    per = chunk // piece
    chunks = selected // chunk
    length = groups * count

    loads = [
        pltpu.make_async_copy(s, d, load_sem.at[i])
        for i, (s, d) in enumerate(((chain_hbm, chain_f), (map_hbm, map_f), (table_hbm, table)))
    ]
    for load in loads:
        load.start()

    barrier = pltpu.get_barrier_semaphore()
    for d in range(1, groups):
        pl.semaphore_signal(
            barrier, inc=1, device_id=(lax.rem(me + d, groups), z), device_id_type=MESH
        )

    @pl.when(z > 0)
    def _():
        pl.semaphore_signal(barrier, inc=1, device_id=(me, z - 1), device_id_type=MESH)

    @pl.when(z < space - 1)
    def _():
        pl.semaphore_signal(barrier, inc=1, device_id=(me, z + 1), device_id_type=MESH)

    if piece < chunk:
        for ref in (i_stage, l_stage, i_recv, l_recv):
            ref[...] = jnp.zeros_like(ref)
    for g in range(groups):
        i_stage[g, :, :, :piece] = inter_ref[:, :, g * piece : (g + 1) * piece]
    i_recv[me] = i_stage[me]

    beside = jnp.where(z > 0, 1, 0) + jnp.where(z < space - 1, 1, 0)
    pl.semaphore_wait(barrier, groups - 1 + beside)

    def hop(src):
        return pltpu.make_async_remote_copy(
            src_ref=src, dst_ref=incoming, send_sem=hop_send, recv_sem=hop_recv,
            device_id=(me, z + 1), device_id_type=MESH,
        )

    def exchange(stage, recv, send_sem, recv_sem, peer):
        return pltpu.make_async_remote_copy(
            src_ref=stage.at[peer], dst_ref=recv.at[me], send_sem=send_sem.at[peer],
            recv_sem=recv_sem.at[me], device_id=(peer, z), device_id_type=MESH,
        )

    def arrival(stage, recv, send_sem, recv_sem, peer):
        return pltpu.make_async_remote_copy(
            src_ref=stage.at[peer], dst_ref=recv.at[peer], send_sem=send_sem.at[peer],
            recv_sem=recv_sem.at[peer], device_id=(peer, z), device_id_type=MESH,
        )

    @pl.when(z == 0)
    def _():
        outgoing[...] = source_ref[...]
        hop(outgoing).start()

    for d in range(1, groups):
        exchange(i_stage, i_recv, i_send, i_got, lax.rem(me + d, groups)).start()

    def prepare():
        loads[1].wait()
        for plane in range(2):
            map_hi[plane], map_lo[plane] = split(map_f[plane])
        row = lax.broadcasted_iota(jnp.int32, (width, chunk), 0)
        for c in range(chunks):
            for side in range(2):
                index = pairs_ref[side : side + 1, c * chunk : (c + 1) * chunk]
                onehot[c, :, side * chunk : (side + 1) * chunk] = jnp.where(
                    row == index, 1.0, 0.0
                ).astype(bf16)

    loads[0].wait()
    for plane in range(2):
        chain_hi[plane], chain_lo[plane] = split(chain_f[plane])

    @pl.when(z >= 2)
    def _():
        prepare()

    @pl.when(z == 0)
    def _():
        incoming[...] = jnp.zeros_like(incoming)

    @pl.when(z > 0)
    def _():
        hop(outgoing).wait_recv()

    def joined():
        return jnp.concatenate([incoming[0], incoming[1]], axis=0)

    @pl.when(jnp.logical_and(z > 0, z < space - 1))
    def _():
        re, im = apply_map(joined(), chain_hi, chain_lo)
        outgoing[0] = re + source_ref[0]
        outgoing[1] = im + source_ref[1]
        hop(outgoing).start()

    @pl.when(z < 2)
    def _():
        prepare()

    re, im = apply_map(joined(), map_hi, map_lo)
    waves = jnp.concatenate([re + local_ref[0], im + local_ref[1]], axis=0)
    rows = jnp.concatenate(split(waves), axis=0)

    for d in range(chunks):
        c = lax.rem((me * piece) // chunk + 1 + d, chunks)
        both = mm(rows, onehot[c])
        both = both[: 2 * count] + both[2 * count :]
        left_re, left_im = both[:count, :chunk], both[count:, :chunk]
        right_re, right_im = both[:count, chunk:], both[count:, chunk:]
        lesser_re = left_re * right_re + left_im * right_im
        lesser_im = left_im * right_re - left_re * right_im
        for j in range(per):
            g = c * per + j
            part = slice(j * piece, (j + 1) * piece)
            l_stage[g, 0, :, :piece] = lesser_re[:, part]
            l_stage[g, 1, :, :piece] = lesser_im[:, part]

            @pl.when(g != me)
            def _():
                exchange(l_stage, l_recv, l_send, l_got, g).start()

            @pl.when(g == me)
            def _():
                l_recv[me] = l_stage[me]

    inner = min(length, RADIX)

    def gathered(recv):
        planes = [recv[:, plane].reshape(length, chunk) for plane in range(2)]
        return [
            (planes[0][a * inner : (a + 1) * inner], planes[1][a * inner : (a + 1) * inner])
            for a in range(length // inner)
        ]

    loads[2].wait()
    for d in range(1, groups):
        arrival(i_stage, i_recv, i_send, i_got, lax.rem(me + groups - d, groups)).wait_recv()
    screened = forward(table[...], gathered(i_recv), length)

    for d in range(1, groups):
        arrival(l_stage, l_recv, l_send, l_got, lax.rem(me + groups - d, groups)).wait_recv()
    lesser = forward(table[...], gathered(l_recv), length)
    spectra = [
        (a * c - b * d, a * d + b * c) for (a, b), (c, d) in zip(lesser, screened)
    ]
    response = inverse(table[...], spectra, length)
    factor = length**-1.5
    share = inner // count
    for a, pair in enumerate(response):
        for plane in range(2):
            r_stage[a * share : (a + 1) * share, plane] = (pair[plane] * factor).reshape(
                share, count, chunk
            )
    for d in range(1, groups):
        exchange(r_stage, r_recv, r_send, r_got, lax.rem(me + d, groups)).start()
    r_recv[me] = r_stage[me]
    for d in range(1, groups):
        arrival(r_stage, r_recv, r_send, r_got, lax.rem(me + groups - d, groups)).wait_recv()
    for g in range(groups):
        out_ref[:, :, g * piece : (g + 1) * piece] = r_recv[g, :, :, :piece]

    for d in range(1, groups):
        peer = lax.rem(me + d, groups)
        exchange(i_stage, i_recv, i_send, i_got, peer).wait_send()
        exchange(l_stage, l_recv, l_send, l_got, peer).wait_send()
        exchange(r_stage, r_recv, r_send, r_got, peer).wait_send()

    @pl.when(z < space - 1)
    def _():
        hop(outgoing).wait_send()


def body(groups, space, chain_map, chain_source, local_map, local_source, interaction, element_pairs):
    count = chain_source.shape[1]
    block = chain_map.shape[2]
    width = local_map.shape[2]
    selected = interaction.shape[1]
    chunk = max(LANES, selected // groups)
    table = jnp.asarray(transform_tables(groups * count))
    exchanged = pltpu.VMEM((groups, 2, count, chunk), f32)
    vmem = pl.BlockSpec(memory_space=pltpu.VMEM)
    hbm = pl.BlockSpec(memory_space=pl.ANY)
    dma = pltpu.SemaphoreType.DMA
    out = pl.pallas_call(
        functools.partial(kernel, groups, space),
        out_shape=jax.ShapeDtypeStruct((2, count, selected), f32),
        in_specs=[hbm, vmem, hbm, vmem, vmem, vmem, hbm],
        out_specs=vmem,
        scratch_shapes=[
            pltpu.VMEM(chain_map.shape, f32),
            pltpu.VMEM(local_map.shape, f32),
            pltpu.VMEM(table.shape, bf16),
            pltpu.VMEM(chain_map.shape, bf16),
            pltpu.VMEM(chain_map.shape, bf16),
            pltpu.VMEM(local_map.shape, bf16),
            pltpu.VMEM(local_map.shape, bf16),
            pltpu.VMEM((selected // chunk, width, 2 * chunk), bf16),
            pltpu.VMEM((2, count, block), f32),
            pltpu.VMEM((2, count, block), f32),
            *[exchanged] * 6,
            dma((3,)),
            dma,
            dma,
            *[dma((groups,))] * 6,
        ],
        compiler_params=pltpu.CompilerParams(
            collective_id=0, has_side_effects=True, vmem_limit_bytes=56 * 2**20
        ),
    )(
        chain_map,
        chain_source,
        local_map,
        jnp.swapaxes(local_source, 1, 2),
        jnp.swapaxes(interaction, 1, 2),
        element_pairs,
        table,
    )
    return jnp.swapaxes(out, 1, 2)


def solution(mesh):
    in_specs = (
        P(None, "space", None),
        P(None, "energy", "space"),
        P(None, "space", None),
        P(None, "space", "energy"),
        P(None, "space", "energy"),
        P(None, "space"),
    )
    out_specs = P(None, "space", "energy")
    run = functools.partial(body, mesh.shape["energy"], mesh.shape["space"])
    return jax.shard_map(run, mesh=mesh, in_specs=in_specs, out_specs=out_specs, check_vma=False)
```

```python
import functools
import math

import jax
import jax.numpy as jnp
import ml_dtypes
import numpy as np
from jax import lax
from jax.experimental import pallas as pl
from jax.experimental.pallas import tpu as pltpu
from jax.sharding import PartitionSpec as P

LANES = 128
RADIX = 256
MESH = pl.DeviceIdType.MESH
bf16, f32 = jnp.bfloat16, jnp.float32


def split(x):
    high = x.astype(bf16)
    return high, (x - high.astype(f32)).astype(bf16)


def mm(a, b):
    return jnp.dot(a, b, preferred_element_type=f32)


def transform_tables(length):
    inner = min(length, RADIX)
    index = np.arange(inner)
    angle = 2.0 * np.pi / inner * (np.outer(index, index) % inner)
    table = np.concatenate([np.cos(angle), np.sin(angle)], axis=0).astype(np.float32)
    high = table.astype(ml_dtypes.bfloat16)
    low = (table - high.astype(np.float32)).astype(ml_dtypes.bfloat16)
    return np.concatenate([high, high, low], axis=1)


def small_transform(table, x, sign):
    inner, width = x.shape[0], x.shape[1] // 2
    high, low = split(x)
    product = mm(table, jnp.concatenate([high, low, high], axis=0))
    cos, sin = product[:inner], product[inner:]
    re = cos[:, :width] - sign * sin[:, width:]
    im = cos[:, width:] + sign * sin[:, :width]
    return re, im


def twiddle(k, inner, length, sign):
    row = lax.broadcasted_iota(jnp.int32, (inner, 1), 0)
    angle = (sign * 2.0 * math.pi / length) * ((row * k) % length).astype(f32)
    return jnp.cos(angle), jnp.sin(angle)


def combine(parts, k, sign):
    total_re = total_im = None
    for a, (re, im) in enumerate(parts):
        angle = sign * 2.0 * math.pi * (a * k % len(parts)) / len(parts)
        c, s = math.cos(angle), math.sin(angle)
        one_re, one_im = c * re - s * im, c * im + s * re
        total_re = one_re if a == 0 else total_re + one_re
        total_im = one_im if a == 0 else total_im + one_im
    return total_re, total_im


def forward(table, parts, length):
    outer, inner = len(parts), parts[0][0].shape[0]
    out = []
    for k in range(outer):
        re, im = parts[0] if outer == 1 else combine(parts, k, -1.0)
        if k:
            c, s = twiddle(k, inner, length, -1.0)
            re, im = c * re - s * im, c * im + s * re
        out.append(small_transform(table, jnp.concatenate([re, im], axis=1), -1.0))
    return out


def inverse(table, spectra, length):
    outer, inner = len(spectra), spectra[0][0].shape[0]
    parts = []
    for k, (re, im) in enumerate(spectra):
        re, im = small_transform(table, jnp.concatenate([re, im], axis=1), 1.0)
        if k:
            c, s = twiddle(k, inner, length, 1.0)
            re, im = c * re - s * im, c * im + s * re
        parts.append((re, im))
    if outer == 1:
        return parts
    return [combine(parts, a, 1.0) for a in range(outer)]


def apply_map(states, high_ref, low_ref):
    count = states.shape[0] // 2
    high, low = split(states)
    rows = jnp.concatenate([high, low], axis=0)
    planes = []
    for plane in range(2):
        p = mm(rows, high_ref[plane])
        planes.append(p[: 2 * count] + p[2 * count :] + mm(high, low_ref[plane]))
    re = planes[0][:count] - planes[1][count:]
    im = planes[1][:count] + planes[0][count:]
    return re, im


def kernel(
    groups, space,
    chain_hbm, source_ref, map_hbm, local_ref, inter_ref, pairs_ref, table_hbm,
    out_ref,
    chain_f, map_f, table, chain_hi, chain_lo, map_hi, map_lo, onehot,
    incoming, outgoing, i_stage, i_recv, l_stage, l_recv, r_stage, r_recv,
    load_sem, hop_send, hop_recv, i_send, i_got, l_send, l_got, r_send, r_got,
):
    me = lax.axis_index("energy")
    z = lax.axis_index("space")
    count = source_ref.shape[1]
    width = local_ref.shape[2]
    selected = inter_ref.shape[2]
    piece = selected // groups
    chunk = l_stage.shape[3]
    per = chunk // piece
    chunks = selected // chunk
    length = groups * count
    cores = 2 if chunks % 2 == 0 else 1

    loads = [
        pltpu.make_async_copy(s, d, load_sem.at[i])
        for i, (s, d) in enumerate(((chain_hbm, chain_f), (map_hbm, map_f), (table_hbm, table)))
    ]
    for load in loads:
        load.start()

    barrier = pltpu.get_barrier_semaphore()
    for d in range(1, groups):
        pl.semaphore_signal(
            barrier, inc=1, device_id=(lax.rem(me + d, groups), z), device_id_type=MESH
        )

    @pl.when(z > 0)
    def _():
        pl.semaphore_signal(barrier, inc=1, device_id=(me, z - 1), device_id_type=MESH)

    @pl.when(z < space - 1)
    def _():
        pl.semaphore_signal(barrier, inc=1, device_id=(me, z + 1), device_id_type=MESH)

    if piece < chunk:
        for ref in (i_stage, l_stage, i_recv, l_recv):
            ref[...] = jnp.zeros_like(ref)
    for g in range(groups):
        i_stage[g, :, :, :piece] = inter_ref[:, :, g * piece : (g + 1) * piece]
    i_recv[me] = i_stage[me]

    beside = jnp.where(z > 0, 1, 0) + jnp.where(z < space - 1, 1, 0)
    pl.semaphore_wait(barrier, groups - 1 + beside)

    turns = incoming.shape[0]
    step = count // turns

    def hop(t):
        return pltpu.make_async_remote_copy(
            src_ref=outgoing.at[t], dst_ref=incoming.at[t], send_sem=hop_send.at[t],
            recv_sem=hop_recv.at[t], device_id=(me, z + 1), device_id_type=MESH,
        )

    def exchange(stage, recv, send_sem, recv_sem, peer):
        return pltpu.make_async_remote_copy(
            src_ref=stage.at[peer], dst_ref=recv.at[me], send_sem=send_sem.at[peer],
            recv_sem=recv_sem.at[me], device_id=(peer, z), device_id_type=MESH,
        )

    def arrival(stage, recv, send_sem, recv_sem, peer):
        return pltpu.make_async_remote_copy(
            src_ref=stage.at[peer], dst_ref=recv.at[peer], send_sem=send_sem.at[peer],
            recv_sem=recv_sem.at[peer], device_id=(peer, z), device_id_type=MESH,
        )

    @pl.when(z == 0)
    def _():
        for t in range(turns):
            outgoing[t] = source_ref[:, t * step : (t + 1) * step]
            hop(t).start()

    for d in range(1, groups):
        exchange(i_stage, i_recv, i_send, i_got, lax.rem(me + d, groups)).start()

    def prepare():
        loads[1].wait()
        for plane in range(2):
            map_hi[plane], map_lo[plane] = split(map_f[plane])
        row = lax.broadcasted_iota(jnp.int32, (width, chunk), 0)
        for c in range(chunks):
            for side in range(2):
                index = pairs_ref[side : side + 1, c * chunk : (c + 1) * chunk]
                onehot[c, :, side * chunk : (side + 1) * chunk] = jnp.where(
                    row == index, 1.0, 0.0
                ).astype(bf16)

    loads[0].wait()
    for plane in range(2):
        chain_hi[plane], chain_lo[plane] = split(chain_f[plane])

    @pl.when(z >= 2)
    def _():
        prepare()

    @pl.when(z == 0)
    def _():
        incoming[...] = jnp.zeros_like(incoming)

    @pl.when(jnp.logical_and(z > 0, z < space - 1))
    def _():
        for t in range(turns):
            hop(t).wait_recv()
            states = jnp.concatenate([incoming[t, 0], incoming[t, 1]], axis=0)
            re, im = apply_map(states, chain_hi, chain_lo)
            outgoing[t, 0] = re + source_ref[0, t * step : (t + 1) * step]
            outgoing[t, 1] = im + source_ref[1, t * step : (t + 1) * step]
            hop(t).start()

    @pl.when(jnp.logical_and(z > 0, z == space - 1))
    def _():
        for t in range(turns):
            hop(t).wait_recv()

    @pl.when(z < 2)
    def _():
        prepare()

    joined = [incoming[t, plane] for plane in range(2) for t in range(turns)]
    re, im = apply_map(jnp.concatenate(joined, axis=0), map_hi, map_lo)
    waves = jnp.concatenate([re + local_ref[0], im + local_ref[1]], axis=0)
    rows = jnp.concatenate(split(waves), axis=0)

    for d in range(chunks):
        pair = lax.rem((me * piece) // (chunk * cores) + 1 + d // cores, chunks // cores)
        c = pair * cores + d % cores
        both = mm(rows, onehot[c])
        both = both[: 2 * count] + both[2 * count :]
        left_re, left_im = both[:count, :chunk], both[count:, :chunk]
        right_re, right_im = both[:count, chunk:], both[count:, chunk:]
        lesser_re = left_re * right_re + left_im * right_im
        lesser_im = left_im * right_re - left_re * right_im
        for j in range(per):
            g = c * per + j
            part = slice(j * piece, (j + 1) * piece)
            l_stage[g, 0, :, :piece] = lesser_re[:, part]
            l_stage[g, 1, :, :piece] = lesser_im[:, part]

            @pl.when(g != me)
            def _():
                exchange(l_stage, l_recv, l_send, l_got, g).start()

            @pl.when(g == me)
            def _():
                l_recv[me] = l_stage[me]

    inner = min(length, RADIX)

    def gathered(recv):
        planes = [recv[:, plane].reshape(length, chunk) for plane in range(2)]
        return [
            (planes[0][a * inner : (a + 1) * inner], planes[1][a * inner : (a + 1) * inner])
            for a in range(length // inner)
        ]

    loads[2].wait()
    for d in range(1, groups):
        arrival(i_stage, i_recv, i_send, i_got, lax.rem(me + groups - d, groups)).wait_recv()
    screened = forward(table[...], gathered(i_recv), length)

    for d in range(1, groups):
        arrival(l_stage, l_recv, l_send, l_got, lax.rem(me + groups - d, groups)).wait_recv()
    lesser = forward(table[...], gathered(l_recv), length)
    spectra = [
        (a * c - b * d, a * d + b * c) for (a, b), (c, d) in zip(lesser, screened)
    ]
    response = inverse(table[...], spectra, length)
    factor = length**-1.5
    share = inner // count
    for a, pair in enumerate(response):
        for plane in range(2):
            r_stage[a * share : (a + 1) * share, plane] = (pair[plane] * factor).reshape(
                share, count, chunk
            )
    for d in range(1, groups):
        exchange(r_stage, r_recv, r_send, r_got, lax.rem(me + d, groups)).start()
    r_recv[me] = r_stage[me]
    for d in range(1, groups):
        arrival(r_stage, r_recv, r_send, r_got, lax.rem(me + groups - d, groups)).wait_recv()
    for g in range(groups):
        out_ref[:, :, g * piece : (g + 1) * piece] = r_recv[g, :, :, :piece]

    for d in range(1, groups):
        peer = lax.rem(me + d, groups)
        exchange(i_stage, i_recv, i_send, i_got, peer).wait_send()
        exchange(l_stage, l_recv, l_send, l_got, peer).wait_send()
        exchange(r_stage, r_recv, r_send, r_got, peer).wait_send()

    @pl.when(z < space - 1)
    def _():
        for t in range(turns):
            hop(t).wait_send()


def body(groups, space, chain_map, chain_source, local_map, local_source, interaction, element_pairs):
    count = chain_source.shape[1]
    block = chain_map.shape[2]
    width = local_map.shape[2]
    selected = interaction.shape[1]
    chunk = max(LANES, selected // groups)
    table = jnp.asarray(transform_tables(groups * count))
    turns = 2 if count % 16 == 0 else 1
    exchanged = pltpu.VMEM((groups, 2, count, chunk), f32)
    vmem = pl.BlockSpec(memory_space=pltpu.VMEM)
    hbm = pl.BlockSpec(memory_space=pltpu.MemorySpace.HBM)
    dma = pltpu.SemaphoreType.DMA
    out = pl.pallas_call(
        functools.partial(kernel, groups, space),
        out_shape=jax.ShapeDtypeStruct((2, count, selected), f32),
        in_specs=[hbm, vmem, hbm, vmem, vmem, vmem, hbm],
        out_specs=vmem,
        scratch_shapes=[
            pltpu.VMEM(chain_map.shape, f32),
            pltpu.VMEM(local_map.shape, f32),
            pltpu.VMEM(table.shape, bf16),
            pltpu.VMEM(chain_map.shape, bf16),
            pltpu.VMEM(chain_map.shape, bf16),
            pltpu.VMEM(local_map.shape, bf16),
            pltpu.VMEM(local_map.shape, bf16),
            pltpu.VMEM((selected // chunk, width, 2 * chunk), bf16),
            pltpu.VMEM((turns, 2, count // turns, block), f32),
            pltpu.VMEM((turns, 2, count // turns, block), f32),
            *[exchanged] * 6,
            dma((3,)),
            dma((turns,)),
            dma((turns,)),
            *[dma((groups,))] * 6,
        ],
        compiler_params=pltpu.CompilerParams(
            collective_id=0, has_side_effects=True, vmem_limit_bytes=53 * 2**20
        ),
    )(
        chain_map,
        chain_source,
        local_map,
        jnp.swapaxes(local_source, 1, 2),
        jnp.swapaxes(interaction, 1, 2),
        element_pairs,
        table,
    )
    return jnp.swapaxes(out, 1, 2)


def solution(mesh):
    in_specs = (
        P(None, "space", None),
        P(None, "energy", "space"),
        P(None, "space", None),
        P(None, "space", "energy"),
        P(None, "space", "energy"),
        P(None, "space"),
    )
    out_specs = P(None, "space", "energy")
    run = functools.partial(body, mesh.shape["energy"], mesh.shape["space"])
    return jax.shard_map(run, mesh=mesh, in_specs=in_specs, out_specs=out_specs, check_vma=False)
```

```python
import functools
import math

import jax
import jax.numpy as jnp
import ml_dtypes
import numpy as np
from jax import lax
from jax.experimental import pallas as pl
from jax.experimental.pallas import tpu as pltpu
from jax.sharding import PartitionSpec as P

LANES = 128
RADIX = 256
MESH = pl.DeviceIdType.MESH
bf16, f32 = jnp.bfloat16, jnp.float32


def split(x):
    high = x.astype(bf16)
    return high, (x - high.astype(f32)).astype(bf16)


def mm(a, b):
    return jnp.dot(a, b, preferred_element_type=f32)


def transform_tables(length):
    inner = min(length, RADIX)
    index = np.arange(inner)
    angle = 2.0 * np.pi / inner * (np.outer(index, index) % inner)
    table = np.concatenate([np.cos(angle), np.sin(angle)], axis=0).astype(np.float32)
    high = table.astype(ml_dtypes.bfloat16)
    low = (table - high.astype(np.float32)).astype(ml_dtypes.bfloat16)
    return np.concatenate([high, high, low], axis=1)


def small_transform(table, x, sign):
    inner, width = x.shape[0], x.shape[1] // 2
    high, low = split(x)
    product = mm(table, jnp.concatenate([high, low, high], axis=0))
    cos, sin = product[:inner], product[inner:]
    re = cos[:, :width] - sign * sin[:, width:]
    im = cos[:, width:] + sign * sin[:, :width]
    return re, im


def twiddle(k, inner, length, sign):
    row = lax.broadcasted_iota(jnp.int32, (inner, 1), 0)
    angle = (sign * 2.0 * math.pi / length) * ((row * k) % length).astype(f32)
    return jnp.cos(angle), jnp.sin(angle)


def combine(parts, k, sign):
    total_re = total_im = None
    for a, (re, im) in enumerate(parts):
        angle = sign * 2.0 * math.pi * (a * k % len(parts)) / len(parts)
        c, s = math.cos(angle), math.sin(angle)
        one_re, one_im = c * re - s * im, c * im + s * re
        total_re = one_re if a == 0 else total_re + one_re
        total_im = one_im if a == 0 else total_im + one_im
    return total_re, total_im


def forward(table, parts, length):
    outer, inner = len(parts), parts[0][0].shape[0]
    out = []
    for k in range(outer):
        re, im = parts[0] if outer == 1 else combine(parts, k, -1.0)
        if k:
            c, s = twiddle(k, inner, length, -1.0)
            re, im = c * re - s * im, c * im + s * re
        out.append(small_transform(table, jnp.concatenate([re, im], axis=1), -1.0))
    return out


def inverse(table, spectra, length):
    outer, inner = len(spectra), spectra[0][0].shape[0]
    parts = []
    for k, (re, im) in enumerate(spectra):
        re, im = small_transform(table, jnp.concatenate([re, im], axis=1), 1.0)
        if k:
            c, s = twiddle(k, inner, length, 1.0)
            re, im = c * re - s * im, c * im + s * re
        parts.append((re, im))
    if outer == 1:
        return parts
    return [combine(parts, a, 1.0) for a in range(outer)]


def apply_map(states, high_ref, low_ref):
    count = states.shape[0] // 2
    high, low = split(states)
    rows = jnp.concatenate([high, low], axis=0)
    planes = []
    for plane in range(2):
        p = mm(rows, high_ref[plane])
        planes.append(p[: 2 * count] + p[2 * count :] + mm(high, low_ref[plane]))
    re = planes[0][:count] - planes[1][count:]
    im = planes[1][:count] + planes[0][count:]
    return re, im


def kernel(
    groups, space,
    chain_hbm, source_ref, map_hbm, local_ref, inter_ref, pairs_ref, table_hbm,
    out_ref,
    chain_f, map_f, table, chain_hi, chain_lo, map_hi, map_lo, onehot,
    incoming, outgoing, i_stage, i_recv, l_stage, l_recv, r_stage, r_recv,
    load_sem, hop_send, hop_recv, i_send, i_got, l_send, l_got, r_send, r_got,
):
    me = lax.axis_index("energy")
    z = lax.axis_index("space")
    count = source_ref.shape[1]
    width = local_ref.shape[2]
    selected = inter_ref.shape[2]
    piece = selected // groups
    chunk = l_stage.shape[3]
    per = chunk // piece
    chunks = selected // chunk
    length = groups * count
    cores = 2 if chunks % 2 == 0 else 1

    loads = [
        pltpu.make_async_copy(s, d, load_sem.at[i])
        for i, (s, d) in enumerate(((chain_hbm, chain_f), (map_hbm, map_f), (table_hbm, table)))
    ]
    for load in loads:
        load.start()

    barrier = pltpu.get_barrier_semaphore()
    for d in range(1, groups):
        pl.semaphore_signal(
            barrier, inc=1, device_id=(lax.rem(me + d, groups), z), device_id_type=MESH
        )

    @pl.when(z > 0)
    def _():
        pl.semaphore_signal(barrier, inc=1, device_id=(me, z - 1), device_id_type=MESH)

    @pl.when(z < space - 1)
    def _():
        pl.semaphore_signal(barrier, inc=1, device_id=(me, z + 1), device_id_type=MESH)

    if piece < chunk:
        for ref in (i_stage, l_stage, i_recv, l_recv):
            ref[...] = jnp.zeros_like(ref)
    for g in range(groups):
        i_stage[g, :, :, :piece] = inter_ref[:, :, g * piece : (g + 1) * piece]
    i_recv[me] = i_stage[me]

    beside = jnp.where(z > 0, 1, 0) + jnp.where(z < space - 1, 1, 0)
    pl.semaphore_wait(barrier, groups - 1 + beside)

    turns = incoming.shape[0]
    step = count // turns

    def hop(t):
        return pltpu.make_async_remote_copy(
            src_ref=outgoing.at[t], dst_ref=incoming.at[t], send_sem=hop_send.at[t],
            recv_sem=hop_recv.at[t], device_id=(me, z + 1), device_id_type=MESH,
        )

    def exchange(stage, recv, send_sem, recv_sem, peer):
        return pltpu.make_async_remote_copy(
            src_ref=stage.at[peer], dst_ref=recv.at[me], send_sem=send_sem.at[peer],
            recv_sem=recv_sem.at[me], device_id=(peer, z), device_id_type=MESH,
        )

    def arrival(stage, recv, send_sem, recv_sem, peer):
        return pltpu.make_async_remote_copy(
            src_ref=stage.at[peer], dst_ref=recv.at[peer], send_sem=send_sem.at[peer],
            recv_sem=recv_sem.at[peer], device_id=(peer, z), device_id_type=MESH,
        )

    @pl.when(z == 0)
    def _():
        for t in range(turns):
            outgoing[t] = source_ref[:, t * step : (t + 1) * step]
            hop(t).start()

    for d in range(1, groups):
        exchange(i_stage, i_recv, i_send, i_got, lax.rem(me + d, groups)).start()

    def prepare():
        loads[1].wait()
        for plane in range(2):
            map_hi[plane], map_lo[plane] = split(map_f[plane])
        row = lax.broadcasted_iota(jnp.int32, (width, chunk), 0)
        for c in range(chunks):
            for side in range(2):
                index = pairs_ref[side : side + 1, c * chunk : (c + 1) * chunk]
                onehot[c, :, side * chunk : (side + 1) * chunk] = jnp.where(
                    row == index, 1.0, 0.0
                ).astype(bf16)

    loads[0].wait()
    for plane in range(2):
        chain_hi[plane], chain_lo[plane] = split(chain_f[plane])

    @pl.when(z >= 2)
    def _():
        prepare()

    @pl.when(z == 0)
    def _():
        incoming[...] = jnp.zeros_like(incoming)

    @pl.when(jnp.logical_and(z > 0, z < space - 1))
    def _():
        for t in range(turns):
            hop(t).wait_recv()
            states = jnp.concatenate([incoming[t, 0], incoming[t, 1]], axis=0)
            re, im = apply_map(states, chain_hi, chain_lo)
            outgoing[t, 0] = re + source_ref[0, t * step : (t + 1) * step]
            outgoing[t, 1] = im + source_ref[1, t * step : (t + 1) * step]
            hop(t).start()

    @pl.when(jnp.logical_and(z > 0, z == space - 1))
    def _():
        for t in range(turns):
            hop(t).wait_recv()

    @pl.when(z < 2)
    def _():
        prepare()

    joined = [incoming[t, plane] for plane in range(2) for t in range(turns)]
    re, im = apply_map(jnp.concatenate(joined, axis=0), map_hi, map_lo)
    waves = jnp.concatenate([re + local_ref[0], im + local_ref[1]], axis=0)
    rows = jnp.concatenate(split(waves), axis=0)

    for d in range(chunks):
        pair = lax.rem((me * piece) // (chunk * cores) + 1 + d // cores, chunks // cores)
        c = pair * cores + d % cores
        both = mm(rows, onehot[c])
        both = both[: 2 * count] + both[2 * count :]
        left_re, left_im = both[:count, :chunk], both[count:, :chunk]
        right_re, right_im = both[:count, chunk:], both[count:, chunk:]
        lesser_re = left_re * right_re + left_im * right_im
        lesser_im = left_im * right_re - left_re * right_im
        for j in range(per):
            g = c * per + j
            part = slice(j * piece, (j + 1) * piece)
            l_stage[g, 0, :, :piece] = lesser_re[:, part]
            l_stage[g, 1, :, :piece] = lesser_im[:, part]

            @pl.when(g != me)
            def _():
                exchange(l_stage, l_recv, l_send, l_got, g).start()

            @pl.when(g == me)
            def _():
                l_recv[me] = l_stage[me]

    inner = min(length, RADIX)

    def gathered(recv):
        planes = [recv[:, plane].reshape(length, chunk) for plane in range(2)]
        return [
            (planes[0][a * inner : (a + 1) * inner], planes[1][a * inner : (a + 1) * inner])
            for a in range(length // inner)
        ]

    loads[2].wait()
    for d in range(1, groups):
        arrival(i_stage, i_recv, i_send, i_got, lax.rem(me + groups - d, groups)).wait_recv()
    screened = forward(table[...], gathered(i_recv), length)

    for d in range(1, groups):
        arrival(l_stage, l_recv, l_send, l_got, lax.rem(me + groups - d, groups)).wait_recv()
    lesser = forward(table[...], gathered(l_recv), length)
    spectra = [
        (a * c - b * d, a * d + b * c) for (a, b), (c, d) in zip(lesser, screened)
    ]
    response = inverse(table[...], spectra, length)
    factor = length**-1.5
    share = inner // count
    for a, pair in enumerate(response):
        for plane in range(2):
            r_stage[a * share : (a + 1) * share, plane] = (pair[plane] * factor).reshape(
                share, count, chunk
            )
    for d in range(1, groups):
        exchange(r_stage, r_recv, r_send, r_got, lax.rem(me + d, groups)).start()
    r_recv[me] = r_stage[me]
    for d in range(1, groups):
        arrival(r_stage, r_recv, r_send, r_got, lax.rem(me + groups - d, groups)).wait_recv()
    for g in range(groups):
        out_ref[:, :, g * piece : (g + 1) * piece] = r_recv[g, :, :, :piece]

    for d in range(1, groups):
        peer = lax.rem(me + d, groups)
        exchange(i_stage, i_recv, i_send, i_got, peer).wait_send()
        exchange(l_stage, l_recv, l_send, l_got, peer).wait_send()
        exchange(r_stage, r_recv, r_send, r_got, peer).wait_send()

    @pl.when(z < space - 1)
    def _():
        for t in range(turns):
            hop(t).wait_send()


def body(groups, space, chain_map, chain_source, local_map, local_source, interaction, element_pairs):
    count = chain_source.shape[1]
    block = chain_map.shape[2]
    width = local_map.shape[2]
    selected = interaction.shape[1]
    chunk = max(LANES, selected // groups)
    table = jnp.asarray(transform_tables(groups * count))
    turns = 2 if count % 16 == 0 else 1
    exchanged = pltpu.VMEM((groups, 2, count, chunk), f32)
    vmem = pl.BlockSpec(memory_space=pltpu.VMEM)
    hbm = pl.BlockSpec(memory_space=pltpu.MemorySpace.HBM)
    dma = pltpu.SemaphoreType.DMA
    out = pl.pallas_call(
        functools.partial(kernel, groups, space),
        out_shape=jax.ShapeDtypeStruct((2, count, selected), f32),
        in_specs=[hbm, vmem, hbm, vmem, vmem, vmem, hbm],
        out_specs=vmem,
        scratch_shapes=[
            pltpu.VMEM(chain_map.shape, f32),
            pltpu.VMEM(local_map.shape, f32),
            pltpu.VMEM(table.shape, bf16),
            pltpu.VMEM(chain_map.shape, bf16),
            pltpu.VMEM(chain_map.shape, bf16),
            pltpu.VMEM(local_map.shape, bf16),
            pltpu.VMEM(local_map.shape, bf16),
            pltpu.VMEM((selected // chunk, width, 2 * chunk), bf16),
            pltpu.VMEM((turns, 2, count // turns, block), f32),
            pltpu.VMEM((turns, 2, count // turns, block), f32),
            *[exchanged] * 6,
            dma((3,)),
            dma((turns,)),
            dma((turns,)),
            *[dma((groups,))] * 6,
        ],
        compiler_params=pltpu.CompilerParams(
            collective_id=0, has_side_effects=True, vmem_limit_bytes=56 * 2**20
        ),
    )(
        chain_map,
        chain_source,
        local_map,
        jnp.swapaxes(local_source, 1, 2),
        jnp.swapaxes(interaction, 1, 2),
        element_pairs,
        table,
    )
    return jnp.swapaxes(out, 1, 2)


def solution(mesh):
    in_specs = (
        P(None, "space", None),
        P(None, "energy", "space"),
        P(None, "space", None),
        P(None, "space", "energy"),
        P(None, "space", "energy"),
        P(None, "space"),
    )
    out_specs = P(None, "space", "energy")
    run = functools.partial(body, mesh.shape["energy"], mesh.shape["space"])
    return jax.shard_map(run, mesh=mesh, in_specs=in_specs, out_specs=out_specs, check_vma=False)
```
